32 devices in a mesh: groups: 2 (over y), tm: 16 (over z, x, core).
Axes of the slice: x: 2, y: 2, z: 4, core: 2. Of those that a mesh axis runs over, the one named last changes fastest.
Arguments:
- frames: bfloat16 [4096, 8192], P('tm', 'groups'), parts along dimension 1, may hold values from -6 to 6
- frame_valid: int32 [8192], P(('groups', 'tm')), parts along dimension 0, may hold values 0 or 1
- valid_count: int32 [32], P('groups'), parts along dimension 0, may hold values from 32 to 128, as said below
- block_map: int32 [32, 256], P('groups'), parts along dimension 0, may hold values from 0 to 255, as said below
- offsets: int32 [4, 2], replicated, may hold values from -4 to 4
Outputs:
- cross: float32 [512, 4, 2, 2048], P(('groups', 'tm')), parts along dimension 0
The draws below stay inside these ranges and needn't reach their ends.
There are 2 independent parts, one for each index of `groups`. The reference program is written for one: setup_inputs(seed, part) draws one part's arguments, and reference() takes and returns one part's arrays. A program takes and returns all parts, laid end to end along the dimension named above; an argument that names none is the same for every part. Nothing has to cross between parts.
Inputs may be any that keep to these rules, and one draw needn't show every extreme that they name: `valid_count`: at most half of a tile's pixels are valid. Some tile has exactly 128 valid pixels and another exactly 32 in every draw; the others are spread evenly between the two. `block_map`: each row is a permutation of the pixels of a tile. Row steps lie in -4 to 4.
All inputs are finite; a program needn't handle non-finite values. No bound on the sum of `frame_valid` on one device may be relied on, other than what follows from the above.
Results may differ from the reference program's by a relative error of at most 0.0052.
Values may be sent and summed in bfloat16 or wider, within the bound.
A program may use at most 64 MiB of HBM per device.

```python
import math
import jax
import jax.numpy as jnp
from jax import lax

ROWS = 16
FRAMES = 4096
BAND = 256
REACH = 4
TILES = 16
TILE_PIX = 256
PIX = 4096


def draw_valid_count(key, part):
    spread = jax.random.randint(jax.random.fold_in(key, 11), (TILES,), TILE_PIX // 8, TILE_PIX // 2 + 1)
    fullest = jax.random.randint(jax.random.fold_in(key, 12), (), 0, TILES)
    step = jax.random.randint(jax.random.fold_in(key, 13), (), 1, TILES)
    emptiest = (fullest + step) % TILES
    tile_idx = jnp.arange(TILES)
    counts = jnp.where(tile_idx == fullest, TILE_PIX // 2, spread)
    counts = jnp.where(tile_idx == emptiest, TILE_PIX // 8, counts)
    return counts.astype(jnp.int32)


def draw_block_map(key, part):
    tile_keys = jax.random.split(jax.random.fold_in(key, 21), TILES)
    return jax.vmap(lambda single: jax.random.permutation(single, TILE_PIX))(tile_keys).astype(jnp.int32)


def draw_offsets(key, part):
    row_steps = jax.random.randint(jax.random.fold_in(key, 31), (4,), -REACH, REACH + 1)
    second = jax.random.randint(jax.random.fold_in(key, 32), (), 1, REACH + 1)
    fourth = jax.random.randint(jax.random.fold_in(key, 33), (), -REACH, 0)
    col_steps = jnp.stack([jnp.int32(REACH), second.astype(jnp.int32), jnp.int32(-REACH), fourth.astype(jnp.int32)])
    return jnp.stack([row_steps.astype(jnp.int32), col_steps], axis=1).astype(jnp.int32)


def with_ends(drawn, rng, least, high):
    longest = drawn.shape.index(max(drawn.shape))
    spots = []
    for shift in (0, 1):
        where = [jax.random.randint(jax.random.fold_in(rng, axis), (), 0, length) for axis, length in enumerate(drawn.shape)]
        where[longest] = (where[longest] + shift) % drawn.shape[longest]
        spots.append(tuple(where))
    return drawn.at[spots[0]].set(least).at[spots[1]].set(high)


def steps_of(key, dims, cuts, low, largest):
    level, own = 1.0, jax.random.fold_in(key, 6)
    for axis_at, parts in cuts:
        draws = jnp.exp(jax.random.uniform(jax.random.fold_in(own, axis_at), (parts,), jnp.float32, low / len(cuts), largest / len(cuts)))
        level = level * jnp.repeat(draws, dims[axis_at] // parts).reshape([-1 if axis == axis_at else 1 for axis in range(len(dims))])
    return level


def centred(rng, dims, width, bound, pieces=(), kind=jnp.bfloat16):
    entries = jax.random.normal(rng, dims, jnp.float32) * width
    if len(pieces) > 0:
        entries = steps_of(rng, dims, pieces, -0.22, 0.18) * entries
    return jnp.clip(entries, min=-bound, max=bound).astype(kind)


def setup_inputs(seed: int = 0, part: int = 0) -> dict:
    key_list = jax.random.split(jax.random.key(seed), 6)
    own_keys = jax.random.split(jax.random.fold_in(key_list[5], part), 6)
    return {
        "frames": centred(own_keys[0], (FRAMES, PIX), 1.0, 6.0, ((0, 16),)),
        "frame_valid": with_ends((jax.random.randint(own_keys[1], (FRAMES,), 0, 8) < 7).astype(jnp.int32), jax.random.fold_in(own_keys[1], 1), 0, 1),
        "valid_count": draw_valid_count(jax.random.fold_in(jax.random.fold_in(key_list[5], part), 71), part),
        "block_map": draw_block_map(jax.random.fold_in(jax.random.fold_in(key_list[5], part), 71), part),
        "offsets": draw_offsets(jax.random.fold_in(key_list[5], 71), part),
    }


def table_piece(frames_len, bin_start, band_width):
    frame_idx = jnp.arange(frames_len, dtype=jnp.int32)[:, None]
    bin_idx = bin_start + jnp.arange(band_width, dtype=jnp.int32)[None, :]
    angles = (frame_idx * bin_idx % frames_len).astype(jnp.float32) * (2.0 * math.pi / frames_len)
    scaling = 1.0 / math.sqrt(frames_len)
    return (jnp.concatenate([jnp.cos(angles), -jnp.sin(angles)], axis=1) * scaling).astype(jnp.bfloat16)

def validity(valid_count, block_map):
    tile_count, tile_pix = block_map.shape
    slot_idx = jnp.arange(tile_pix, dtype=jnp.int32)[None, :]
    live = (slot_idx < valid_count[:, None]).astype(jnp.float32)
    tile_idx = jnp.arange(tile_count, dtype=jnp.int32)[:, None]
    return jnp.zeros((tile_count, tile_pix), jnp.float32).at[tile_idx, block_map].set(live)

def cross_block(extended, ext_valid, offsets, tile_width):
    spectra = extended.astype(jnp.float32)
    row_count = spectra.shape[0]
    half = spectra.shape[2] // 2
    padded = jnp.pad(spectra, ((REACH, REACH), (0, 0), (0, 0)))
    padded_valid = jnp.pad(ext_valid, ((REACH, REACH), (0, 0)))
    own_spec = spectra[:, REACH:REACH + tile_width]
    own_valid = ext_valid[:, REACH:REACH + tile_width]
    own_real = own_spec[..., :half]
    own_imag = own_spec[..., half:]
    results = []
    for which in range(offsets.shape[0]):
        row_step = offsets[which, 0] + REACH
        col_step = offsets[which, 1] + REACH
        shifted = lax.dynamic_slice(padded, (row_step, col_step, jnp.int32(0)), (row_count, tile_width, 2 * half))
        shifted_valid = lax.dynamic_slice(padded_valid, (row_step, col_step), (row_count, tile_width))
        other_real = shifted[..., :half]
        other_imag = shifted[..., half:]
        real_part = lax.optimization_barrier(jnp.sum(own_real * other_real + own_imag * other_imag, axis=0))
        imag_part = lax.optimization_barrier(jnp.sum(own_imag * other_real - own_real * other_imag, axis=0))
        pair_count = lax.optimization_barrier(jnp.sum(own_valid * shifted_valid, axis=0))
        scaling = 1.0 / jnp.maximum(pair_count, 1.0)
        results.append(jnp.stack([real_part, imag_part], axis=1) * scaling[:, None, None])
    return jnp.stack(results, axis=1)

def reference(frames, frame_valid, valid_count, block_map, offsets):
    frames_len, pixel_count = frames.shape
    masked = (frames * frame_valid[:, None].astype(frames.dtype)).astype(jnp.float32)
    valid_all = validity(valid_count, block_map)
    tile_count, tile_pix = valid_all.shape
    tile_width = tile_pix // ROWS
    col_count = tile_count * tile_width
    valid_grid = valid_all.reshape(tile_count, ROWS, tile_width).transpose(1, 0, 2).reshape(ROWS, col_count)
    ext_valid = jnp.pad(valid_grid, ((0, 0), (REACH, REACH)))
    pixel_valid = valid_all.reshape(pixel_count)

    def one_band(band_index):
        bin_start = (band_index * BAND).astype(jnp.int32)
        table = table_piece(frames_len, bin_start, BAND).astype(jnp.float32)
        spectra = lax.dot_general(masked, table, (((0,), (0,)), ((), ())), precision=lax.Precision.HIGHEST)
        spectra = (spectra * pixel_valid[:, None]).astype(jnp.bfloat16)
        spectra = spectra.reshape(tile_count, ROWS, tile_width, 2 * BAND).transpose(1, 0, 2, 3)
        spectra = spectra.reshape(ROWS, col_count, 2 * BAND)
        extended = jnp.pad(spectra, ((0, 0), (REACH, REACH), (0, 0)))
        return cross_block(extended, ext_valid, offsets, col_count)
    results = lax.map(one_band, jnp.arange(frames_len // 2 // BAND, dtype=jnp.int32))
    return results.transpose(1, 2, 3, 0, 4).reshape(col_count, offsets.shape[0], 2, frames_len // 2)
```

```python
import functools
import math

import jax
import jax.numpy as jnp
import ml_dtypes
import numpy as np
from jax import lax
from jax.experimental import pallas as pl
from jax.experimental.pallas import tpu as pltpu
from jax.sharding import PartitionSpec as P

ROWS = 16
REACH = 4
RADIX = 16
VMEM_LIMIT = 56 * 1024 * 1024


def dft_table(frames_len):
    span = frames_len // RADIX
    per = span // 2
    j = np.arange(span)
    out = np.zeros((RADIX, 2 * per, 2 * span), np.float64)
    for k1 in range(RADIX):
        bins = k1 + RADIX * np.arange(per)
        angle = (bins[:, None] * j[None, :] % frames_len) * (2.0 * math.pi / frames_len)
        cos, sin = np.cos(angle), np.sin(angle)
        sign = 1.0 if k1 <= RADIX // 2 else -1.0
        out[k1, :per, :span] = cos
        out[k1, :per, span:] = sign * sin
        out[k1, per:, :span] = -sin
        out[k1, per:, span:] = sign * cos
    return (out / math.sqrt(frames_len)).astype(np.float32).astype(ml_dtypes.bfloat16)


def pack_kernel(frames_ref, keep_ref, slots_ref, out_ref):
    tiles, _, slot_count = out_ref.shape
    tile_pix = slots_ref.shape[1]
    keep = keep_ref[...]
    slot_idx = lax.broadcasted_iota(jnp.int32, (slot_count, tile_pix), 0)

    def one_tile(tile, carry):
        row = slots_ref[pl.ds(tile, 1), :]
        pick = (slot_idx == row).astype(jnp.float32).astype(jnp.bfloat16)
        start = pl.multiple_of(tile * tile_pix, tile_pix)
        packed = lax.dot_general(
            frames_ref[:, pl.ds(start, tile_pix)], pick, (((1,), (1,)), ((), ())),
            preferred_element_type=jnp.float32,
        )
        out_ref[tile] = (packed * keep).astype(jnp.bfloat16)
        return carry

    lax.fori_loop(0, tiles, one_tile, 0)


def radix_sixteen(x):
    c1, c2, c3 = (math.cos(math.pi * n / 8.0) for n in (1, 2, 3))
    s = [x[d] + x[d + 8] for d in range(8)]
    t = [x[d] - x[d + 8] for d in range(8)]
    u = [s[d] + s[d + 4] for d in range(4)]
    v = [s[d] - s[d + 4] for d in range(4)]
    z = [None] * 9
    z[0] = (u[0] + u[2] + (u[1] + u[3]), None)
    z[8] = (u[0] + u[2] - (u[1] + u[3]), None)
    z[4] = (u[0] - u[2], u[3] - u[1])
    less, more = c2 * (v[1] - v[3]), c2 * (v[1] + v[3])
    z[2] = (v[0] + less, -(v[2] + more))
    z[6] = (v[0] - less, v[2] - more)
    a1, a2, a3 = t[1] - t[7], c2 * (t[2] - t[6]), t[3] - t[5]
    b1, b2, b3 = t[1] + t[7], c2 * (t[2] + t[6]), t[3] + t[5]
    p, q = t[0] + a2, c1 * a1 + c3 * a3
    z[1], z[7] = [p + q, None], [p - q, None]
    p, q = t[0] - a2, c3 * a1 - c1 * a3
    z[3], z[5] = [p + q, None], [p - q, None]
    p, q = c3 * b1 + c1 * b3, b2 + t[4]
    z[1][1], z[7][1] = -(p + q), q - p
    p, q = c1 * b1 - c3 * b3, b2 - t[4]
    z[3][1], z[5][1] = -(p + q), q - p
    return z


def cross_kernel(own_ref, left_ref, right_ref, table_ref, ids_ref, scale_ref, out_ref,
                 high_ref, low_ref, spec_ref, pick_ref):
    frames_len, slot_count = own_ref.shape
    span = frames_len // RADIX
    per = span // 2
    step_rows = 16
    half = slot_count // 2
    total = 2 * slot_count

    id_lane = lax.broadcasted_iota(jnp.int32, pick_ref.shape, 1)
    pick_ref[...] = (ids_ref[...] == id_lane).astype(jnp.float32).astype(jnp.bfloat16)

    lane = lax.broadcasted_iota(jnp.int32, (step_rows, slot_count), 1)
    front = lane < half

    def put(k1, part, start, lane0, value):
        if value is None:
            value = jnp.zeros((step_rows, slot_count), jnp.float32)
        high = value.astype(jnp.bfloat16)
        low = (value - high.astype(jnp.float32)).astype(jnp.bfloat16)
        rows = pl.ds(part * span + start, step_rows)
        high_ref[k1, rows, lane0:lane0 + slot_count] = high
        low_ref[k1, rows, lane0:lane0 + slot_count] = low

    def one_step(step, carry):
        start = pl.multiple_of(step * step_rows, step_rows)
        own, near = [], [None] * RADIX
        for d in range(RADIX):
            own.append(own_ref[pl.ds(d * span + start, step_rows), :].astype(jnp.float32))
        for d in range(RADIX // 2):
            left = left_ref[pl.ds(d * span + start, step_rows), :].astype(jnp.float32)
            right = right_ref[pl.ds(d * span + start, step_rows), :].astype(jnp.float32)
            near[d] = jnp.where(front, left, pltpu.roll(right, half, 1))
            near[d + 8] = jnp.where(front, pltpu.roll(left, half, 1), right)
        for lane0, group in ((0, own), (slot_count, near)):
            for k1, (real, imag) in enumerate(radix_sixteen(group)):
                put(k1, 0, start, lane0, real)
                put(k1, 1, start, lane0, imag)
        return carry

    lax.fori_loop(0, span // step_rows, one_step, 0)

    for k1 in range(RADIX):
        src = min(k1, RADIX - k1)
        found = jnp.dot(table_ref[k1], high_ref[src], preferred_element_type=jnp.float32)
        found = found + jnp.dot(table_ref[k1], low_ref[src], preferred_element_type=jnp.float32)
        for side in range(2):
            lanes = slice(side * slot_count, (side + 1) * slot_count)
            for part in range(2):
                spec_ref[part, side, pl.ds(k1, per, RADIX), :] = found[part * per:(part + 1) * per, lanes]

    bins = RADIX * per
    width = 256
    pix = ids_ref.shape[0] // 5
    cols = pix // ROWS

    def one_band(band, carry):
        start = pl.multiple_of(band * width, width)
        grids = []
        for part in range(2):
            spec = jnp.concatenate(
                [spec_ref[part, side, pl.ds(start, width), :] for side in range(2)], axis=1
            ).astype(jnp.bfloat16)
            grids.append(lax.dot_general(
                pick_ref[...], spec, (((1,), (1,)), ((), ())), preferred_element_type=jnp.float32
            ))
        real, imag = grids
        own_r, own_i = real[:pix], imag[:pix]
        for which in range(4):
            rows = slice((which + 1) * pix, (which + 2) * pix)
            far_r, far_i = real[rows], imag[rows]
            scale = scale_ref[which]
            out_r = jnp.sum((own_r * far_r + own_i * far_i).reshape(ROWS, cols, width), axis=0)
            out_i = jnp.sum((own_i * far_r - own_r * far_i).reshape(ROWS, cols, width), axis=0)
            out_ref[:, which, 0, pl.ds(start, width)] = out_r * scale
            out_ref[:, which, 1, pl.ds(start, width)] = out_i * scale
        return carry

    lax.fori_loop(0, bins // width, one_band, 0)


def slot_numbers(valid_count, block_map):
    tile_pix = block_map.shape[1]
    tile_width = tile_pix // ROWS
    idx = jnp.arange(tile_pix, dtype=jnp.int32)
    live = idx[None, :] < valid_count[:, None]
    match = (block_map[:, :, None] == idx[None, None, :]) & live[:, :, None]
    valid = jnp.any(match, axis=1)
    col = idx % tile_width
    order = col * ROWS + idx // tile_width
    before = (order[:, None] < order[None, :]).astype(jnp.bfloat16)
    rank = jnp.dot(valid.astype(jnp.bfloat16), before, preferred_element_type=jnp.float32).astype(jnp.int32)
    shift = jnp.where(col[None, :] >= tile_width // 2, tile_pix // 2 - valid_count[:, None], 0)
    return jnp.where(valid, rank + shift, -1)


def pair_ids(slots, offsets, position):
    tile_pix = slots.shape[1]
    tile_width = tile_pix // ROWS
    half = tile_pix // 4
    padded = jnp.pad(slots, ((1, 1), (0, 0)), constant_values=-1)
    near = lax.dynamic_slice_in_dim(padded, position, 3, 0).reshape(3, ROWS, tile_width)
    left = near[0][:, tile_width - REACH:]
    right = near[2][:, :REACH]
    left = jnp.where(left >= 0, left + half, -1)
    right = jnp.where(right >= 0, right + 3 * half, -1)
    grid = jnp.concatenate([left, near[1], right], axis=1)
    grid = jnp.pad(grid, ((REACH, REACH), (0, 0)), constant_values=-1)
    own = near[1]
    ids, scales = [own], []
    for which in range(offsets.shape[0]):
        far = lax.dynamic_slice(
            grid, (offsets[which, 0] + REACH, offsets[which, 1] + REACH), (ROWS, tile_width)
        )
        ids.append(far)
        pairs = jnp.sum(((own >= 0) & (far >= 0)).astype(jnp.float32), axis=0)
        scales.append(1.0 / jnp.maximum(pairs, 1.0))
    return jnp.stack(ids).reshape(-1, 1), jnp.stack(scales)[:, :, None]


def per_device(table, frames, frame_valid, valid_count, block_map, offsets):
    tile_count = lax.axis_size("tm")
    position = lax.axis_index("tm")
    frame_dev, pixel_count = frames.shape
    tile_pix = pixel_count // tile_count
    tile_width = tile_pix // ROWS
    slot_count = tile_pix // 2
    half = slot_count // 2
    frames_len = tile_count * frame_dev
    slots = slot_numbers(valid_count, block_map)
    keep = frame_valid.astype(jnp.float32)[:, None]
    packed = pl.pallas_call(
        pack_kernel,
        out_shape=jax.ShapeDtypeStruct((tile_count, frame_dev, slot_count), jnp.bfloat16),
        compiler_params=pltpu.CompilerParams(vmem_limit_bytes=VMEM_LIMIT),
        name="pack_valid",
    )(frames, keep, slots)
    own = lax.all_to_all(packed, "tm", split_axis=0, concat_axis=0, tiled=True)
    own = own.reshape(frames_len, slot_count)
    mid = frames_len // 2
    to_left = jnp.concatenate([own[:mid, :half], own[mid:, :half]], axis=1)
    to_right = jnp.concatenate([own[:mid, half:], own[mid:, half:]], axis=1)
    right = lax.ppermute(to_left, "tm", [(i + 1, i) for i in range(tile_count - 1)])
    left = lax.ppermute(to_right, "tm", [(i, i + 1) for i in range(tile_count - 1)])
    ids, scales = pair_ids(slots, offsets, position)
    span = frames_len // RADIX
    bins = frames_len // 2
    return pl.pallas_call(
        cross_kernel,
        out_shape=jax.ShapeDtypeStruct((tile_width, offsets.shape[0], 2, bins), jnp.float32),
        scratch_shapes=[
            pltpu.VMEM((RADIX // 2 + 1, 2 * span, 2 * slot_count), jnp.bfloat16),
            pltpu.VMEM((RADIX // 2 + 1, 2 * span, 2 * slot_count), jnp.bfloat16),
            pltpu.VMEM((2, 2, bins, slot_count), jnp.float32),
            pltpu.VMEM((5 * tile_pix, 2 * slot_count), jnp.bfloat16),
        ],
        compiler_params=pltpu.CompilerParams(vmem_limit_bytes=VMEM_LIMIT),
        name="transform_cross",
    )(own, left, right, table, ids, scales)


def solution(mesh):
    def run(frames, frame_valid, valid_count, block_map, offsets):
        table = jnp.asarray(dft_table(frames.shape[0]))
        return jax.shard_map(
            per_device,
            mesh=mesh,
            in_specs=(P(), P("tm", "groups"), P(("groups", "tm")), P("groups"), P("groups", None), P()),
            out_specs=P(("groups", "tm"), None, None, None),
            check_vma=False,
        )(table, frames, frame_valid, valid_count, block_map, offsets)

    return run
```

```python
import functools
import math

import jax
import jax.numpy as jnp
import ml_dtypes
import numpy as np
from jax import lax
from jax.experimental import pallas as pl
from jax.experimental.pallas import tpu as pltpu
from jax.sharding import PartitionSpec as P

ROWS = 16
REACH = 4
RADIX = 16
VMEM_LIMIT = 56 * 1024 * 1024


def dft_table(frames_len):
    span = frames_len // RADIX
    per = span // 2
    j = np.arange(span)
    out = np.zeros((RADIX, 2 * per, 2 * span), np.float64)
    for k1 in range(RADIX):
        bins = k1 + RADIX * np.arange(per)
        angle = (bins[:, None] * j[None, :] % frames_len) * (2.0 * math.pi / frames_len)
        cos, sin = np.cos(angle), np.sin(angle)
        sign = 1.0 if k1 <= RADIX // 2 else -1.0
        out[k1, :per, :span] = cos
        out[k1, :per, span:] = sign * sin
        out[k1, per:, :span] = -sin
        out[k1, per:, span:] = sign * cos
    return (out / math.sqrt(frames_len)).astype(np.float32).astype(ml_dtypes.bfloat16)


def bits(flags):
    return flags.astype(jnp.float32).astype(jnp.bfloat16)


def dot_last(left, right):
    return lax.dot_general(
        left, right, (((1,), (1,)), ((), ())), preferred_element_type=jnp.float32
    )


def number_slots(count_ref, map_ref, slots_ref):
    tiles, tile_pix = map_ref.shape
    width = tile_pix // ROWS
    shift = width.bit_length() - 1
    group = tile_pix // ROWS
    row_idx = lax.broadcasted_iota(jnp.int32, (tile_pix, tile_pix), 0)
    col_idx = lax.broadcasted_iota(jnp.int32, (tile_pix, tile_pix), 1)
    row_high, row_low = row_idx >> shift, row_idx & (width - 1)
    col_high, col_low = col_idx >> shift, col_idx & (width - 1)
    same_tile = row_high == col_high
    same_low = bits(row_low == col_low)
    row_match = row_low == col_high
    before = bits(row_low * ROWS + row_high < col_low * ROWS + col_high)
    slim = lax.broadcasted_iota(jnp.int32, (group, tile_pix), 0)
    lane = lax.broadcasted_iota(jnp.int32, (group, tile_pix), 1)
    tile_pick = bits((lane >> shift) == slim)
    part_idx = lax.broadcasted_iota(jnp.int32, (group, ROWS, tile_pix), 1)
    for first in range(0, tiles, group):
        count = count_ref[first:first + group, :]
        pixel = map_ref[first:first + group, :]
        row = jnp.where(lane < count, pixel >> shift, -1)
        col = pixel & (width - 1)
        row_hot = (row[:, None, :] == part_idx).astype(jnp.float32).reshape(tile_pix, tile_pix)
        col_hot = (col[:, None, :] == part_idx).astype(jnp.float32).reshape(tile_pix, tile_pix)
        met = dot_last(row_hot.astype(jnp.bfloat16), col_hot.astype(jnp.bfloat16))
        met = jnp.where(same_tile, met, 0.0).astype(jnp.bfloat16)
        wide = jnp.dot(met, same_low, preferred_element_type=jnp.float32)
        wide = jnp.where(row_match, wide, 0.0).astype(jnp.bfloat16)
        valid = jnp.dot(tile_pick, wide, preferred_element_type=jnp.float32)
        rank = jnp.dot(valid.astype(jnp.bfloat16), before, preferred_element_type=jnp.float32)
        back = jnp.where((lane & (width - 1)) >= width // 2, tile_pix // 2 - count, 0)
        slots_ref[first:first + group, :] = jnp.where(
            valid > 0.5, rank.astype(jnp.int32) + back, -1
        )


def pick_pairs(me, tiles, slots_ref, offsets_ref, pick_ref, scale_ref):
    tile_pix = slots_ref.shape[1]
    width = tile_pix // ROWS
    shift = width.bit_length() - 1
    quarter = tile_pix // 4
    left = slots_ref[pl.ds((me + tiles - 1) % tiles, 1), :]
    own = slots_ref[pl.ds(me, 1), :]
    right = slots_ref[pl.ds((me + 1) % tiles, 1), :]
    left = jnp.where((left >= quarter * 1) & (me > 0), left + quarter, -1)
    right = jnp.where((right >= 0) & (right < quarter) & (me < tiles - 1), right + 3 * quarter, -1)
    row_idx = lax.broadcasted_iota(jnp.int32, (tile_pix, tile_pix), 0)
    col_idx = lax.broadcasted_iota(jnp.int32, (tile_pix, tile_pix), 1)
    sides = [bits(row_idx == ids) for ids in (left, own, right)]
    own_valid = None
    for which in range(5):
        row, col = row_idx >> shift, row_idx & (width - 1)
        if which > 0:
            row = row + offsets_ref[which - 1, 0]
            col = col + offsets_ref[which - 1, 1]
        here = ((row * width + (col & (width - 1))) == col_idx) & (row >= 0) & (row < ROWS)
        conds = (col < 0, (col >= 0) & (col < width), col >= width)
        found = None
        for cond, side in zip(conds, sides):
            term = dot_last(bits(here & cond), side)
            found = term if found is None else found + term
        pick_ref[which * tile_pix:(which + 1) * tile_pix, :] = found.astype(jnp.bfloat16)
        valid = jnp.sum(found, axis=1, keepdims=True)
        if which == 0:
            own_valid = valid
        else:
            both = jnp.broadcast_to(own_valid * valid, (tile_pix, 128)).reshape(ROWS, width, 128)
            scale_ref[which - 1] = 1.0 / jnp.maximum(jnp.sum(both, axis=0), 1.0)


def exchange_kernel(tiles, frames_ref, keep_ref, count_ref, map_ref, offsets_ref,
                    own_ref, left_ref, right_ref, pick_ref, scale_ref,
                    slots_ref, pack_ref, side_ref, send_sem, recv_sem, halo_send, halo_recv):
    me = lax.axis_index("tm")
    group = lax.axis_index("groups")
    rows = pack_ref.shape[1]
    slot_count = pack_ref.shape[2]
    tile_pix = slots_ref.shape[1]
    half_tiles = tiles // 2
    half = slot_count // 2
    mesh_id = pl.DeviceIdType.MESH

    barrier = pltpu.get_barrier_semaphore()

    def greet(step, carry):
        pl.semaphore_signal(
            barrier, inc=1, device_id=(group, (me + step) % tiles), device_id_type=mesh_id
        )
        return carry

    lax.fori_loop(1, tiles, greet, 0)

    number_slots(count_ref, map_ref, slots_ref)
    keep = jnp.broadcast_to(keep_ref[...].astype(jnp.float32), (slot_count, rows)).T
    slot_idx = lax.broadcasted_iota(jnp.int32, (slot_count, tile_pix), 0)

    def packed(tile):
        pick = bits(slot_idx == slots_ref[pl.ds(tile, 1), :])
        start = pl.multiple_of(tile * tile_pix, tile_pix)
        return (dot_last(frames_ref[:, pl.ds(start, tile_pix)], pick) * keep).astype(jnp.bfloat16)

    def block(source):
        return pl.ds(pl.multiple_of(source * rows, rows), rows)

    def to_owner(tile, source):
        return pltpu.make_async_remote_copy(
            src_ref=pack_ref.at[tile], dst_ref=own_ref.at[block(source)],
            send_sem=send_sem.at[tile], recv_sem=recv_sem.at[source],
            device_id=(group, tile), device_id_type=mesh_id,
        )

    pl.semaphore_wait(barrier, tiles - 1)

    def send(tile):
        pack_ref[tile] = packed(tile)
        to_owner(tile, me).start()

    send((me + half_tiles) % tiles)

    def send_two(step, carry):
        send((me + half_tiles + step) % tiles)
        send((me + step) % tiles)
        return carry

    lax.fori_loop(1, half_tiles, send_two, 0)
    own_ref[block(me), :] = packed(me)
    pick_pairs(me, tiles, slots_ref, offsets_ref, pick_ref, scale_ref)

    def to_side(way, source):
        target = (me + tiles - 1) % tiles if way == 0 else (me + 1) % tiles
        dst = right_ref if way == 0 else left_ref
        return pltpu.make_async_remote_copy(
            src_ref=side_ref.at[way, block(source)], dst_ref=dst.at[block(source)],
            send_sem=halo_send.at[way, source], recv_sem=halo_recv.at[way, source],
            device_id=(group, target), device_id_type=mesh_id,
        )

    has_left, has_right = me > 0, me < tiles - 1

    def forward(step, carry):
        low = (me + tiles - step) % half_tiles
        high = low + half_tiles
        for source in (low, high):
            @pl.when(source != me)
            def _():
                to_owner((me + 1) % tiles, source).wait_recv()
        near, far = own_ref[block(low), :], own_ref[block(high), :]
        side_ref[0, block(low), :] = jnp.concatenate([near[:, :half], far[:, :half]], axis=1)
        side_ref[1, block(low), :] = jnp.concatenate([near[:, half:], far[:, half:]], axis=1)

        @pl.when(has_left)
        def _():
            to_side(0, low).start()

        @pl.when(has_right)
        def _():
            to_side(1, low).start()

        return carry

    lax.fori_loop(0, half_tiles, forward, 0)

    @pl.when(me == 0)
    def _():
        left_ref[...] = jnp.zeros_like(left_ref)

    @pl.when(me == tiles - 1)
    def _():
        right_ref[...] = jnp.zeros_like(right_ref)

    def sent(step, carry):
        to_owner((me + step) % tiles, me).wait_send()
        return carry

    lax.fori_loop(1, tiles, sent, 0)

    def arrived(source, carry):
        @pl.when(has_left)
        def _():
            to_side(0, source).wait_send()
            to_side(1, source).wait_recv()

        @pl.when(has_right)
        def _():
            to_side(1, source).wait_send()
            to_side(0, source).wait_recv()

        return carry

    lax.fori_loop(0, half_tiles, arrived, 0)


def radix_sixteen(x):
    c1, c2, c3 = (math.cos(math.pi * n / 8.0) for n in (1, 2, 3))
    s = [x[d] + x[d + 8] for d in range(8)]
    t = [x[d] - x[d + 8] for d in range(8)]
    u = [s[d] + s[d + 4] for d in range(4)]
    v = [s[d] - s[d + 4] for d in range(4)]
    z = [None] * 9
    z[0] = (u[0] + u[2] + (u[1] + u[3]), None)
    z[8] = (u[0] + u[2] - (u[1] + u[3]), None)
    z[4] = (u[0] - u[2], u[3] - u[1])
    less, more = c2 * (v[1] - v[3]), c2 * (v[1] + v[3])
    z[2] = (v[0] + less, -(v[2] + more))
    z[6] = (v[0] - less, v[2] - more)
    a1, a2, a3 = t[1] - t[7], c2 * (t[2] - t[6]), t[3] - t[5]
    b1, b2, b3 = t[1] + t[7], c2 * (t[2] + t[6]), t[3] + t[5]
    p, q = t[0] + a2, c1 * a1 + c3 * a3
    z[1], z[7] = [p + q, None], [p - q, None]
    p, q = t[0] - a2, c3 * a1 - c1 * a3
    z[3], z[5] = [p + q, None], [p - q, None]
    p, q = c3 * b1 + c1 * b3, b2 + t[4]
    z[1][1], z[7][1] = -(p + q), q - p
    p, q = c1 * b1 - c3 * b3, b2 - t[4]
    z[3][1], z[5][1] = -(p + q), q - p
    return z


def cross_kernel(own_ref, left_ref, right_ref, table_ref, pick_ref, scale_ref, out_ref,
                 high_ref, spec_ref):
    frames_len, slot_count = own_ref.shape
    span = frames_len // RADIX
    per = span // 2
    step_rows = 16
    half = slot_count // 2

    lane = lax.broadcasted_iota(jnp.int32, (step_rows, slot_count), 1)
    front = lane < half

    def put(k1, part, start, lane0, value):
        if value is not None:
            rows = pl.ds(part * span + start, step_rows)
            high_ref[k1, rows, lane0:lane0 + slot_count] = value.astype(jnp.bfloat16)

    def one_step(step, carry):
        start = pl.multiple_of(step * step_rows, step_rows)
        own, near = [], [None] * RADIX
        for d in range(RADIX):
            own.append(own_ref[pl.ds(d * span + start, step_rows), :].astype(jnp.float32))
        for d in range(RADIX // 2):
            left = left_ref[pl.ds(d * span + start, step_rows), :].astype(jnp.float32)
            right = right_ref[pl.ds(d * span + start, step_rows), :].astype(jnp.float32)
            near[d] = jnp.where(front, left, pltpu.roll(right, half, 1))
            near[d + 8] = jnp.where(front, pltpu.roll(left, half, 1), right)
        for lane0, group in ((0, own), (slot_count, near)):
            for k1, (real, imag) in enumerate(radix_sixteen(group)):
                put(k1, 0, start, lane0, real)
                put(k1, 1, start, lane0, imag)
        return carry

    lax.fori_loop(0, span // step_rows, one_step, 0)

    for k1 in range(RADIX):
        src = min(k1, RADIX - k1)
        depth = span if k1 % (RADIX // 2) == 0 else 2 * span
        found = jnp.dot(
            table_ref[k1, :, :depth], high_ref[src, :depth, :], preferred_element_type=jnp.float32
        )
        for side in range(2):
            lanes = slice(side * slot_count, (side + 1) * slot_count)
            for part in range(2):
                spec_ref[part, side, pl.ds(k1, per, RADIX), :] = found[part * per:(part + 1) * per, lanes]

    bins = RADIX * per
    width = 256
    pix = pick_ref.shape[0] // 5
    cols = pix // ROWS

    def one_band(band, carry):
        start = pl.multiple_of(band * width, width)
        grids = []
        for part in range(2):
            spec = jnp.concatenate(
                [spec_ref[part, side, pl.ds(start, width), :] for side in range(2)], axis=1
            ).astype(jnp.bfloat16)
            grids.append(lax.dot_general(
                pick_ref[...], spec, (((1,), (1,)), ((), ())), preferred_element_type=jnp.float32
            ))
        real, imag = grids
        own_r, own_i = real[:pix], imag[:pix]
        for which in range(4):
            rows = slice((which + 1) * pix, (which + 2) * pix)
            far_r, far_i = real[rows], imag[rows]
            scale = jnp.concatenate([scale_ref[which]] * (width // 128), axis=1)
            out_r = jnp.sum((own_r * far_r + own_i * far_i).reshape(ROWS, cols, width), axis=0)
            out_i = jnp.sum((own_i * far_r - own_r * far_i).reshape(ROWS, cols, width), axis=0)
            out_ref[:, which, 0, pl.ds(start, width)] = out_r * scale
            out_ref[:, which, 1, pl.ds(start, width)] = out_i * scale
        return carry

    lax.fori_loop(0, bins // width, one_band, 0)


def per_device(table, frames, frame_valid, valid_count, block_map, offsets):
    tile_count = lax.axis_size("tm")
    frame_dev, pixel_count = frames.shape
    tile_pix = pixel_count // tile_count
    tile_width = tile_pix // ROWS
    slot_count = tile_pix // 2
    frames_len = tile_count * frame_dev
    span = frames_len // RADIX
    bins = frames_len // 2
    vmem = pl.BlockSpec(memory_space=pltpu.VMEM)
    own, left, right, pick, scales = pl.pallas_call(
        functools.partial(exchange_kernel, tile_count),
        out_shape=[
            jax.ShapeDtypeStruct((frames_len, slot_count), jnp.bfloat16),
            jax.ShapeDtypeStruct((bins, slot_count), jnp.bfloat16),
            jax.ShapeDtypeStruct((bins, slot_count), jnp.bfloat16),
            jax.ShapeDtypeStruct((5 * tile_pix, tile_pix), jnp.bfloat16),
            jax.ShapeDtypeStruct((offsets.shape[0], tile_width, 128), jnp.float32),
        ],
        in_specs=[vmem] * 4 + [pl.BlockSpec(memory_space=pltpu.SMEM)],
        out_specs=[vmem] * 5,
        scratch_shapes=[
            pltpu.VMEM((tile_count, tile_pix), jnp.int32),
            pltpu.VMEM((tile_count, frame_dev, slot_count), jnp.bfloat16),
            pltpu.VMEM((2, bins, slot_count), jnp.bfloat16),
            pltpu.SemaphoreType.DMA((tile_count,)),
            pltpu.SemaphoreType.DMA((tile_count,)),
            pltpu.SemaphoreType.DMA((2, tile_count // 2)),
            pltpu.SemaphoreType.DMA((2, tile_count // 2)),
        ],
        compiler_params=pltpu.CompilerParams(
            vmem_limit_bytes=VMEM_LIMIT, collective_id=0, has_side_effects=True
        ),
        name="exchange",
    )(frames, frame_valid[None, :], valid_count[:, None], block_map, offsets)
    return pl.pallas_call(
        cross_kernel,
        out_shape=jax.ShapeDtypeStruct((tile_width, offsets.shape[0], 2, bins), jnp.float32),
        scratch_shapes=[
            pltpu.VMEM((RADIX // 2 + 1, 2 * span, 2 * slot_count), jnp.bfloat16),
            pltpu.VMEM((2, 2, bins, slot_count), jnp.float32),
        ],
        compiler_params=pltpu.CompilerParams(vmem_limit_bytes=VMEM_LIMIT),
        name="transform_cross",
    )(own, left, right, table, pick, scales)


def solution(mesh):
    def run(frames, frame_valid, valid_count, block_map, offsets):
        table = jnp.asarray(dft_table(frames.shape[0]))
        return jax.shard_map(
            per_device,
            mesh=mesh,
            in_specs=(P(), P("tm", "groups"), P(("groups", "tm")), P("groups"), P("groups", None), P()),
            out_specs=P(("groups", "tm"), None, None, None),
            check_vma=False,
        )(table, frames, frame_valid, valid_count, block_map, offsets)

    return run
```

```python
import functools
import math

import jax
import jax.numpy as jnp
import ml_dtypes
import numpy as np
from jax import lax
from jax.experimental import pallas as pl
from jax.experimental.pallas import tpu as pltpu
from jax.sharding import PartitionSpec as P

ROWS = 16
REACH = 4
RADIX = 16
EXCHANGE_VMEM = 24 * 1024 * 1024
CROSS_VMEM = 36 * 1024 * 1024


def dft_table(frames_len):
    span = frames_len // RADIX
    per = span // 2
    j = np.arange(span)
    out = np.zeros((RADIX, 2 * per, 2 * span), np.float64)
    for k1 in range(RADIX):
        bins = k1 + RADIX * np.arange(per)
        angle = (bins[:, None] * j[None, :] % frames_len) * (2.0 * math.pi / frames_len)
        cos, sin = np.cos(angle), np.sin(angle)
        sign = 1.0 if k1 <= RADIX // 2 else -1.0
        out[k1, :per, :span] = cos
        out[k1, :per, span:] = sign * sin
        out[k1, per:, :span] = -sin
        out[k1, per:, span:] = sign * cos
    return (out / math.sqrt(frames_len)).astype(np.float32).astype(ml_dtypes.bfloat16)


def bits(flags):
    return flags.astype(jnp.float32).astype(jnp.bfloat16)


def dot_last(left, right):
    return lax.dot_general(
        left, right, (((1,), (1,)), ((), ())), preferred_element_type=jnp.float32
    )


def number_slots(count_ref, map_ref, slots_ref):
    tiles, tile_pix = map_ref.shape
    width = tile_pix // ROWS
    shift = width.bit_length() - 1
    group = tile_pix // ROWS
    row_idx = lax.broadcasted_iota(jnp.int32, (tile_pix, tile_pix), 0)
    col_idx = lax.broadcasted_iota(jnp.int32, (tile_pix, tile_pix), 1)
    row_high, row_low = row_idx >> shift, row_idx & (width - 1)
    col_high, col_low = col_idx >> shift, col_idx & (width - 1)
    same_tile = row_high == col_high
    same_low = bits(row_low == col_low)
    row_match = row_low == col_high
    before = bits(row_low * ROWS + row_high < col_low * ROWS + col_high)
    slim = lax.broadcasted_iota(jnp.int32, (group, tile_pix), 0)
    lane = lax.broadcasted_iota(jnp.int32, (group, tile_pix), 1)
    tile_pick = bits((lane >> shift) == slim)
    part_idx = lax.broadcasted_iota(jnp.int32, (group, ROWS, tile_pix), 1)
    for first in range(0, tiles, group):
        near_diag = lax.broadcasted_iota(jnp.int32, (group, tiles), 1) == (
            lax.broadcasted_iota(jnp.int32, (group, tiles), 0) + first
        )
        count = jnp.sum(
            jnp.where(near_diag, count_ref[...].astype(jnp.float32), 0.0), axis=1, keepdims=True
        ).astype(jnp.int32)
        pixel = map_ref[first:first + group, :]
        row = jnp.where(lane < count, pixel >> shift, -1)
        col = pixel & (width - 1)
        row_hot = (row[:, None, :] == part_idx).astype(jnp.float32).reshape(tile_pix, tile_pix)
        col_hot = (col[:, None, :] == part_idx).astype(jnp.float32).reshape(tile_pix, tile_pix)
        met = dot_last(row_hot.astype(jnp.bfloat16), col_hot.astype(jnp.bfloat16))
        met = jnp.where(same_tile, met, 0.0).astype(jnp.bfloat16)
        wide = jnp.dot(met, same_low, preferred_element_type=jnp.float32)
        wide = jnp.where(row_match, wide, 0.0).astype(jnp.bfloat16)
        valid = jnp.dot(tile_pick, wide, preferred_element_type=jnp.float32)
        rank = jnp.dot(valid.astype(jnp.bfloat16), before, preferred_element_type=jnp.float32)
        back = jnp.where((lane & (width - 1)) >= width // 2, tile_pix // 2 - count, 0)
        slots_ref[first:first + group, :] = jnp.where(
            valid > 0.5, rank.astype(jnp.int32) + back, -1
        )


def pick_pairs(me, tiles, slots_ref, offsets_ref, pick_ref, scale_ref):
    tile_pix = slots_ref.shape[1]
    width = tile_pix // ROWS
    shift = width.bit_length() - 1
    quarter = tile_pix // 4
    left = slots_ref[pl.ds((me + tiles - 1) % tiles, 1), :]
    own = slots_ref[pl.ds(me, 1), :]
    right = slots_ref[pl.ds((me + 1) % tiles, 1), :]
    left = jnp.where((left >= quarter * 1) & (me > 0), left + quarter, -1)
    right = jnp.where((right >= 0) & (right < quarter) & (me < tiles - 1), right + 3 * quarter, -1)
    row_idx = lax.broadcasted_iota(jnp.int32, (tile_pix, tile_pix), 0)
    col_idx = lax.broadcasted_iota(jnp.int32, (tile_pix, tile_pix), 1)
    sides = [bits(row_idx == ids) for ids in (left, own, right)]
    own_valid = None
    for which in range(5):
        row, col = row_idx >> shift, row_idx & (width - 1)
        if which > 0:
            row = row + offsets_ref[0:1, which - 1:which]
            col = col + offsets_ref[1:2, which - 1:which]
        here = ((row * width + (col & (width - 1))) == col_idx) & (row >= 0) & (row < ROWS)
        conds = (col < 0, (col >= 0) & (col < width), col >= width)
        found = None
        for cond, side in zip(conds, sides):
            term = dot_last(bits(here & cond), side)
            found = term if found is None else found + term
        pick_ref[which * tile_pix:(which + 1) * tile_pix, :] = found.astype(jnp.bfloat16)
        valid = jnp.sum(found, axis=1, keepdims=True)
        if which == 0:
            own_valid = valid
        else:
            both = jnp.broadcast_to(own_valid * valid, (tile_pix, 128)).reshape(ROWS, width, 128)
            scale_ref[which - 1] = 1.0 / jnp.maximum(jnp.sum(both, axis=0), 1.0)


def exchange_kernel(tiles, frames_ref, keep_ref, count_ref, map_ref, offsets_ref,
                    own_ref, left_ref, right_ref, pick_ref, scale_ref,
                    slots_ref, pack_ref, side_ref, fold_ref, direct_ref,
                    send_sem, recv_sem, halo_send, halo_recv, direct_send, direct_recv):
    me = lax.axis_index("tm")
    group = lax.axis_index("groups")
    rows = pack_ref.shape[1]
    slot_count = pack_ref.shape[2]
    tile_pix = slots_ref.shape[1]
    half_tiles = tiles // 2
    half = slot_count // 2
    mesh_id = pl.DeviceIdType.MESH

    barrier = pltpu.get_barrier_semaphore()

    def greet(step, carry):
        pl.semaphore_signal(
            barrier, inc=1, device_id=(group, (me + step) % tiles), device_id_type=mesh_id
        )
        return carry

    lax.fori_loop(1, tiles, greet, 0)

    number_slots(count_ref, map_ref, slots_ref)
    keep = jnp.broadcast_to(keep_ref[...].astype(jnp.float32), (slot_count, rows)).T
    slot_idx = lax.broadcasted_iota(jnp.int32, (slot_count, tile_pix), 0)

    def packed(tile):
        pick = bits(slot_idx == slots_ref[pl.ds(tile, 1), :])
        start = pl.multiple_of(tile * tile_pix, tile_pix)
        return (dot_last(frames_ref[:, pl.ds(start, tile_pix)], pick) * keep).astype(jnp.bfloat16)

    def block(source):
        return pl.ds(pl.multiple_of(source * rows, rows), rows)

    def to_owner(tile, source):
        return pltpu.make_async_remote_copy(
            src_ref=pack_ref.at[tile], dst_ref=own_ref.at[block(source)],
            send_sem=send_sem.at[tile], recv_sem=recv_sem.at[source],
            device_id=(group, tile), device_id_type=mesh_id,
        )

    pl.semaphore_wait(barrier, tiles - 1)

    def send(tile):
        pack_ref[tile] = packed(tile)
        to_owner(tile, me).start()

    send((me + half_tiles) % tiles)

    def send_two(step, carry):
        send((me + half_tiles + step) % tiles)
        send((me + step) % tiles)
        return carry

    lax.fori_loop(1, half_tiles, send_two, 0)
    pack_ref[me] = packed(me)
    own_ref[block(me), :] = pack_ref[me]

    mid = half_tiles - 1
    mids = (mid, mid + 1)

    def to_mid(which, source):
        return pltpu.make_async_remote_copy(
            src_ref=fold_ref.at[which], dst_ref=direct_ref.at[source],
            send_sem=direct_send.at[which], recv_sem=direct_recv.at[source],
            device_id=(group, mids[which]), device_id_type=mesh_id,
        )

    for which in range(2):
        block_there = pack_ref[mids[1 - which]]
        lanes = slice(0, half) if which == 0 else slice(half, slot_count)
        margin = block_there[:, lanes]
        fold_ref[which] = jnp.concatenate([margin[:rows // 2], margin[rows // 2:]], axis=1)

        @pl.when(me != mids[which])
        def _():
            to_mid(which, me).start()

        @pl.when(me == mids[which])
        def _():
            direct_ref[me] = fold_ref[which]

    pick_pairs(me, tiles, slots_ref, offsets_ref, pick_ref, scale_ref)

    def to_side(way, source):
        target = (me + tiles - 1) % tiles if way == 0 else (me + 1) % tiles
        dst = right_ref if way == 0 else left_ref
        return pltpu.make_async_remote_copy(
            src_ref=side_ref.at[way, block(source)], dst_ref=dst.at[block(source)],
            send_sem=halo_send.at[way, source], recv_sem=halo_recv.at[way, source],
            device_id=(group, target), device_id_type=mesh_id,
        )

    has_left = (me > 0) & (me != half_tiles)
    has_right = (me < tiles - 1) & (me != half_tiles - 1)

    def forward(step, carry):
        low = (me + tiles - step) % half_tiles
        high = low + half_tiles
        for source in (low, high):
            @pl.when(source != me)
            def _():
                to_owner((me + 1) % tiles, source).wait_recv()
        near, far = own_ref[block(low), :], own_ref[block(high), :]
        side_ref[0, block(low), :] = jnp.concatenate([near[:, :half], far[:, :half]], axis=1)
        side_ref[1, block(low), :] = jnp.concatenate([near[:, half:], far[:, half:]], axis=1)

        @pl.when(has_left)
        def _():
            to_side(0, low).start()

        @pl.when(has_right)
        def _():
            to_side(1, low).start()

        return carry

    lax.fori_loop(0, half_tiles, forward, 0)

    @pl.when(me == 0)
    def _():
        left_ref[...] = jnp.zeros_like(left_ref)

    @pl.when(me == tiles - 1)
    def _():
        right_ref[...] = jnp.zeros_like(right_ref)

    for which, dst in ((0, right_ref), (1, left_ref)):
        @pl.when(me == mids[which])
        def _():
            def unfold(low, carry):
                parts = []
                for source in (low, low + half_tiles):
                    @pl.when(source != me)
                    def _():
                        to_mid(1 - which, source).wait_recv()
                    fold = direct_ref[source]
                    parts.append(jnp.concatenate([fold[:, :half], fold[:, half:]], axis=0))
                dst[block(low), :] = jnp.concatenate(parts, axis=1)
                return carry

            lax.fori_loop(0, half_tiles, unfold, 0)

        @pl.when(me != mids[which])
        def _():
            to_mid(which, me).wait_send()

    def sent(step, carry):
        to_owner((me + step) % tiles, me).wait_send()
        return carry

    lax.fori_loop(1, tiles, sent, 0)

    def arrived(source, carry):
        @pl.when(has_left)
        def _():
            to_side(0, source).wait_send()
            to_side(1, source).wait_recv()

        @pl.when(has_right)
        def _():
            to_side(1, source).wait_send()
            to_side(0, source).wait_recv()

        return carry

    lax.fori_loop(0, half_tiles, arrived, 0)


def radix_sixteen(x):
    c1, c2, c3 = (math.cos(math.pi * n / 8.0) for n in (1, 2, 3))
    s = [x[d] + x[d + 8] for d in range(8)]
    t = [x[d] - x[d + 8] for d in range(8)]
    u = [s[d] + s[d + 4] for d in range(4)]
    v = [s[d] - s[d + 4] for d in range(4)]
    z = [None] * 9
    z[0] = (u[0] + u[2] + (u[1] + u[3]), None)
    z[8] = (u[0] + u[2] - (u[1] + u[3]), None)
    z[4] = (u[0] - u[2], u[3] - u[1])
    less, more = c2 * (v[1] - v[3]), c2 * (v[1] + v[3])
    z[2] = (v[0] + less, -(v[2] + more))
    z[6] = (v[0] - less, v[2] - more)
    a1, a2, a3 = t[1] - t[7], c2 * (t[2] - t[6]), t[3] - t[5]
    b1, b2, b3 = t[1] + t[7], c2 * (t[2] + t[6]), t[3] + t[5]
    p, q = t[0] + a2, c1 * a1 + c3 * a3
    z[1], z[7] = [p + q, None], [p - q, None]
    p, q = t[0] - a2, c3 * a1 - c1 * a3
    z[3], z[5] = [p + q, None], [p - q, None]
    p, q = c3 * b1 + c1 * b3, b2 + t[4]
    z[1][1], z[7][1] = -(p + q), q - p
    p, q = c1 * b1 - c3 * b3, b2 - t[4]
    z[3][1], z[5][1] = -(p + q), q - p
    return z


def cross_kernel(own_ref, left_ref, right_ref, table_ref, pick_ref, scale_ref, out_ref,
                 high_ref, spec_ref):
    frames_len, slot_count = own_ref.shape
    span = frames_len // RADIX
    per = span // 2
    step_rows = 16
    half = slot_count // 2

    lane = lax.broadcasted_iota(jnp.int32, (step_rows, slot_count), 1)
    front = lane < half

    def put(k1, part, start, lane0, value):
        if value is not None:
            rows = pl.ds(part * span + start, step_rows)
            high_ref[k1, rows, lane0:lane0 + slot_count] = value.astype(jnp.bfloat16)

    def one_step(step, carry):
        start = pl.multiple_of(step * step_rows, step_rows)
        own, near = [], [None] * RADIX
        for d in range(RADIX):
            own.append(own_ref[pl.ds(d * span + start, step_rows), :].astype(jnp.float32))
        for d in range(RADIX // 2):
            left = left_ref[pl.ds(d * span + start, step_rows), :].astype(jnp.float32)
            right = right_ref[pl.ds(d * span + start, step_rows), :].astype(jnp.float32)
            near[d] = jnp.where(front, left, pltpu.roll(right, half, 1))
            near[d + 8] = jnp.where(front, pltpu.roll(left, half, 1), right)
        for lane0, group in ((0, own), (slot_count, near)):
            for k1, (real, imag) in enumerate(radix_sixteen(group)):
                put(k1, 0, start, lane0, real)
                put(k1, 1, start, lane0, imag)
        return carry

    lax.fori_loop(0, span // step_rows, one_step, 0)

    for k1 in range(RADIX):
        src = min(k1, RADIX - k1)
        depth = span if k1 % (RADIX // 2) == 0 else 2 * span
        found = jnp.dot(
            table_ref[k1, :, :depth], high_ref[src, :depth, :], preferred_element_type=jnp.float32
        )
        for side in range(2):
            lanes = slice(side * slot_count, (side + 1) * slot_count)
            for part in range(2):
                spec_ref[part, side, pl.ds(k1, per, RADIX), :] = found[part * per:(part + 1) * per, lanes]

    bins = RADIX * per
    width = 256
    pix = pick_ref.shape[0] // 5
    cols = pix // ROWS

    def one_band(band, carry):
        start = pl.multiple_of(band * width, width)
        grids = []
        for part in range(2):
            spec = jnp.concatenate(
                [spec_ref[part, side, pl.ds(start, width), :] for side in range(2)], axis=1
            ).astype(jnp.bfloat16)
            grids.append(lax.dot_general(
                pick_ref[...], spec, (((1,), (1,)), ((), ())), preferred_element_type=jnp.float32
            ))
        real, imag = grids
        own_r, own_i = real[:pix], imag[:pix]
        for which in range(4):
            rows = slice((which + 1) * pix, (which + 2) * pix)
            far_r, far_i = real[rows], imag[rows]
            scale = jnp.concatenate([scale_ref[which]] * (width // 128), axis=1)
            out_r = jnp.sum((own_r * far_r + own_i * far_i).reshape(ROWS, cols, width), axis=0)
            out_i = jnp.sum((own_i * far_r - own_r * far_i).reshape(ROWS, cols, width), axis=0)
            out_ref[:, which, 0, pl.ds(start, width)] = out_r * scale
            out_ref[:, which, 1, pl.ds(start, width)] = out_i * scale
        return carry

    lax.fori_loop(0, bins // width, one_band, 0)


def per_device(table, frames, frame_valid, valid_count, block_map, offsets):
    tile_count = lax.axis_size("tm")
    frame_dev, pixel_count = frames.shape
    tile_pix = pixel_count // tile_count
    tile_width = tile_pix // ROWS
    slot_count = tile_pix // 2
    frames_len = tile_count * frame_dev
    span = frames_len // RADIX
    bins = frames_len // 2
    vmem = pl.BlockSpec(memory_space=pltpu.VMEM)
    own, left, right, pick, scales = pl.pallas_call(
        functools.partial(exchange_kernel, tile_count),
        out_shape=[
            jax.ShapeDtypeStruct((frames_len, slot_count), jnp.bfloat16),
            jax.ShapeDtypeStruct((bins, slot_count), jnp.bfloat16),
            jax.ShapeDtypeStruct((bins, slot_count), jnp.bfloat16),
            jax.ShapeDtypeStruct((5 * tile_pix, tile_pix), jnp.bfloat16),
            jax.ShapeDtypeStruct((offsets.shape[0], tile_width, 128), jnp.float32),
        ],
        in_specs=[vmem] * 5,
        out_specs=[vmem] * 5,
        scratch_shapes=[
            pltpu.VMEM((tile_count, tile_pix), jnp.int32),
            pltpu.VMEM((tile_count, frame_dev, slot_count), jnp.bfloat16),
            pltpu.VMEM((2, bins, slot_count), jnp.bfloat16),
            pltpu.VMEM((2, frame_dev // 2, slot_count), jnp.bfloat16),
            pltpu.VMEM((tile_count, frame_dev // 2, slot_count), jnp.bfloat16),
            pltpu.SemaphoreType.DMA((tile_count,)),
            pltpu.SemaphoreType.DMA((tile_count,)),
            pltpu.SemaphoreType.DMA((2, tile_count // 2)),
            pltpu.SemaphoreType.DMA((2, tile_count // 2)),
            pltpu.SemaphoreType.DMA((2,)),
            pltpu.SemaphoreType.DMA((tile_count,)),
        ],
        compiler_params=pltpu.CompilerParams(
            vmem_limit_bytes=EXCHANGE_VMEM, collective_id=0, has_side_effects=True
        ),
        name="exchange",
    )(frames, frame_valid[None, :], valid_count[None, :], block_map, offsets.T)
    return pl.pallas_call(
        cross_kernel,
        out_shape=jax.ShapeDtypeStruct((tile_width, offsets.shape[0], 2, bins), jnp.float32),
        scratch_shapes=[
            pltpu.VMEM((RADIX // 2 + 1, 2 * span, 2 * slot_count), jnp.bfloat16),
            pltpu.VMEM((2, 2, bins, slot_count), jnp.float32),
        ],
        compiler_params=pltpu.CompilerParams(vmem_limit_bytes=CROSS_VMEM),
        name="transform_cross",
    )(own, left, right, table, pick, scales)


def solution(mesh):
    def run(frames, frame_valid, valid_count, block_map, offsets):
        table = jnp.asarray(dft_table(frames.shape[0]))
        return jax.shard_map(
            per_device,
            mesh=mesh,
            in_specs=(P(), P("tm", "groups"), P(("groups", "tm")), P("groups"), P("groups", None), P()),
            out_specs=P(("groups", "tm"), None, None, None),
            check_vma=False,
        )(table, frames, frame_valid, valid_count, block_map, offsets)

    return run
```

```python
import functools
import math

import jax
import jax.numpy as jnp
import ml_dtypes
import numpy as np
from jax import lax
from jax.experimental import pallas as pl
from jax.experimental.pallas import tpu as pltpu
from jax.sharding import PartitionSpec as P

ROWS = 16
REACH = 4
RADIX = 16
VMEM_LIMIT = 56 * 1024 * 1024


def dft_table(frames_len):
    span = frames_len // RADIX
    per = span // 2
    j = np.arange(span)
    out = np.zeros((RADIX, 2 * per, 2 * span), np.float64)
    for k1 in range(RADIX):
        bins = k1 + RADIX * np.arange(per)
        angle = (bins[:, None] * j[None, :] % frames_len) * (2.0 * math.pi / frames_len)
        cos, sin = np.cos(angle), np.sin(angle)
        sign = 1.0 if k1 <= RADIX // 2 else -1.0
        out[k1, :per, :span] = cos
        out[k1, :per, span:] = sign * sin
        out[k1, per:, :span] = -sin
        out[k1, per:, span:] = sign * cos
    return (out / math.sqrt(frames_len)).astype(np.float32).astype(ml_dtypes.bfloat16)


def bits(flags):
    return flags.astype(jnp.float32).astype(jnp.bfloat16)


def dot_last(left, right):
    return lax.dot_general(
        left, right, (((1,), (1,)), ((), ())), preferred_element_type=jnp.float32
    )


def number_slots(count_ref, map_ref, slots_ref):
    tiles, tile_pix = map_ref.shape
    width = tile_pix // ROWS
    shift = width.bit_length() - 1
    group = tile_pix // ROWS
    row_idx = lax.broadcasted_iota(jnp.int32, (tile_pix, tile_pix), 0)
    col_idx = lax.broadcasted_iota(jnp.int32, (tile_pix, tile_pix), 1)
    row_high, row_low = row_idx >> shift, row_idx & (width - 1)
    col_high, col_low = col_idx >> shift, col_idx & (width - 1)
    same_tile = row_high == col_high
    same_low = bits(row_low == col_low)
    row_match = row_low == col_high
    before = bits(row_low * ROWS + row_high < col_low * ROWS + col_high)
    slim = lax.broadcasted_iota(jnp.int32, (group, tile_pix), 0)
    lane = lax.broadcasted_iota(jnp.int32, (group, tile_pix), 1)
    tile_pick = bits((lane >> shift) == slim)
    part_idx = lax.broadcasted_iota(jnp.int32, (group, ROWS, tile_pix), 1)
    for first in range(0, tiles, group):
        near_diag = lax.broadcasted_iota(jnp.int32, (group, tiles), 1) == (
            lax.broadcasted_iota(jnp.int32, (group, tiles), 0) + first
        )
        count = jnp.sum(
            jnp.where(near_diag, count_ref[...].astype(jnp.float32), 0.0), axis=1, keepdims=True
        ).astype(jnp.int32)
        pixel = map_ref[first:first + group, :]
        row = jnp.where(lane < count, pixel >> shift, -1)
        col = pixel & (width - 1)
        row_hot = (row[:, None, :] == part_idx).astype(jnp.float32).reshape(tile_pix, tile_pix)
        col_hot = (col[:, None, :] == part_idx).astype(jnp.float32).reshape(tile_pix, tile_pix)
        met = dot_last(row_hot.astype(jnp.bfloat16), col_hot.astype(jnp.bfloat16))
        met = jnp.where(same_tile, met, 0.0).astype(jnp.bfloat16)
        wide = jnp.dot(met, same_low, preferred_element_type=jnp.float32)
        wide = jnp.where(row_match, wide, 0.0).astype(jnp.bfloat16)
        valid = jnp.dot(tile_pick, wide, preferred_element_type=jnp.float32)
        rank = jnp.dot(valid.astype(jnp.bfloat16), before, preferred_element_type=jnp.float32)
        back = jnp.where((lane & (width - 1)) >= width // 2, tile_pix // 2 - count, 0)
        slots_ref[first:first + group, :] = jnp.where(
            valid > 0.5, rank.astype(jnp.int32) + back, -1
        )


def pick_pairs(me, tiles, slots_ref, offsets_ref, pick_ref, scale_ref):
    tile_pix = slots_ref.shape[1]
    width = tile_pix // ROWS
    shift = width.bit_length() - 1
    quarter = tile_pix // 4
    left = slots_ref[pl.ds((me + tiles - 1) % tiles, 1), :]
    own = slots_ref[pl.ds(me, 1), :]
    right = slots_ref[pl.ds((me + 1) % tiles, 1), :]
    left = jnp.where((left >= quarter * 1) & (me > 0), left + quarter, -1)
    right = jnp.where((right >= 0) & (right < quarter) & (me < tiles - 1), right + 3 * quarter, -1)
    row_idx = lax.broadcasted_iota(jnp.int32, (tile_pix, tile_pix), 0)
    col_idx = lax.broadcasted_iota(jnp.int32, (tile_pix, tile_pix), 1)
    sides = [bits(row_idx == ids) for ids in (left, own, right)]
    own_valid = None
    for which in range(5):
        row, col = row_idx >> shift, row_idx & (width - 1)
        if which > 0:
            row = row + offsets_ref[0:1, which - 1:which]
            col = col + offsets_ref[1:2, which - 1:which]
        here = ((row * width + (col & (width - 1))) == col_idx) & (row >= 0) & (row < ROWS)
        conds = (col < 0, (col >= 0) & (col < width), col >= width)
        found = None
        for cond, side in zip(conds, sides):
            term = dot_last(bits(here & cond), side)
            found = term if found is None else found + term
        pick_ref[which * tile_pix:(which + 1) * tile_pix, :] = found.astype(jnp.bfloat16)
        valid = jnp.sum(found, axis=1, keepdims=True)
        if which == 0:
            own_valid = valid
        else:
            both = jnp.broadcast_to(own_valid * valid, (tile_pix, 128)).reshape(ROWS, width, 128)
            scale_ref[which - 1] = 1.0 / jnp.maximum(jnp.sum(both, axis=0), 1.0)


def exchange_kernel(tiles, far_ref, keep_ref, count_ref, map_ref, offsets_ref,
                    own_ref, left_ref, right_ref, pick_ref, scale_ref,
                    frames_ref, slots_ref, pack_ref, side_ref, fold_ref, direct_ref,
                    send_sem, recv_sem, halo_send, halo_recv, direct_send, direct_recv,
                    load_sem):
    me = lax.axis_index("tm")
    group = lax.axis_index("groups")
    rows = pack_ref.shape[1]
    slot_count = pack_ref.shape[2]
    tile_pix = slots_ref.shape[1]
    half_tiles = tiles // 2
    half = slot_count // 2
    mesh_id = pl.DeviceIdType.MESH

    load = pltpu.make_async_copy(far_ref, frames_ref, load_sem)
    load.start()
    barrier = pltpu.get_barrier_semaphore()

    def greet(step, carry):
        pl.semaphore_signal(
            barrier, inc=1, device_id=(group, (me + step) % tiles), device_id_type=mesh_id
        )
        return carry

    lax.fori_loop(1, tiles, greet, 0)

    number_slots(count_ref, map_ref, slots_ref)
    keep = jnp.broadcast_to(keep_ref[...].astype(jnp.float32), (slot_count, rows)).T
    slot_idx = lax.broadcasted_iota(jnp.int32, (slot_count, tile_pix), 0)

    def packed(tile):
        pick = bits(slot_idx == slots_ref[pl.ds(tile, 1), :])
        start = pl.multiple_of(tile * tile_pix, tile_pix)
        return (dot_last(frames_ref[:, pl.ds(start, tile_pix)], pick) * keep).astype(jnp.bfloat16)

    def block(source):
        return pl.ds(pl.multiple_of(source * rows, rows), rows)

    def to_owner(tile, source):
        return pltpu.make_async_remote_copy(
            src_ref=pack_ref.at[tile], dst_ref=own_ref.at[block(source)],
            send_sem=send_sem.at[tile], recv_sem=recv_sem.at[source],
            device_id=(group, tile), device_id_type=mesh_id,
        )

    load.wait()
    pl.semaphore_wait(barrier, tiles - 1)

    def send(tile):
        pack_ref[tile] = packed(tile)
        to_owner(tile, me).start()

    send((me + half_tiles) % tiles)

    def send_two(step, carry):
        send((me + half_tiles + step) % tiles)
        send((me + step) % tiles)
        return carry

    lax.fori_loop(1, half_tiles, send_two, 0)
    pack_ref[me] = packed(me)
    own_ref[block(me), :] = pack_ref[me]

    mid = half_tiles - 1
    mids = (mid, mid + 1)

    def to_mid(which, source):
        return pltpu.make_async_remote_copy(
            src_ref=fold_ref.at[which], dst_ref=direct_ref.at[source],
            send_sem=direct_send.at[which], recv_sem=direct_recv.at[source],
            device_id=(group, mids[which]), device_id_type=mesh_id,
        )

    for which in range(2):
        block_there = pack_ref[mids[1 - which]]
        lanes = slice(0, half) if which == 0 else slice(half, slot_count)
        margin = block_there[:, lanes]
        fold_ref[which] = jnp.concatenate([margin[:rows // 2], margin[rows // 2:]], axis=1)

        @pl.when(me != mids[which])
        def _():
            to_mid(which, me).start()

        @pl.when(me == mids[which])
        def _():
            direct_ref[me] = fold_ref[which]

    pick_pairs(me, tiles, slots_ref, offsets_ref, pick_ref, scale_ref)

    def to_side(way, source):
        target = (me + tiles - 1) % tiles if way == 0 else (me + 1) % tiles
        dst = right_ref if way == 0 else left_ref
        return pltpu.make_async_remote_copy(
            src_ref=side_ref.at[way, block(source)], dst_ref=dst.at[block(source)],
            send_sem=halo_send.at[way, source], recv_sem=halo_recv.at[way, source],
            device_id=(group, target), device_id_type=mesh_id,
        )

    has_left = (me > 0) & (me != half_tiles)
    has_right = (me < tiles - 1) & (me != half_tiles - 1)

    def forward(step, carry):
        low = (me + tiles - step) % half_tiles
        high = low + half_tiles
        for source in (low, high):
            @pl.when(source != me)
            def _():
                to_owner((me + 1) % tiles, source).wait_recv()
        near, far = own_ref[block(low), :], own_ref[block(high), :]
        side_ref[0, block(low), :] = jnp.concatenate([near[:, :half], far[:, :half]], axis=1)
        side_ref[1, block(low), :] = jnp.concatenate([near[:, half:], far[:, half:]], axis=1)

        @pl.when(has_left)
        def _():
            to_side(0, low).start()

        @pl.when(has_right)
        def _():
            to_side(1, low).start()

        return carry

    lax.fori_loop(0, half_tiles, forward, 0)

    @pl.when(me == 0)
    def _():
        left_ref[...] = jnp.zeros_like(left_ref)

    @pl.when(me == tiles - 1)
    def _():
        right_ref[...] = jnp.zeros_like(right_ref)

    for which, dst in ((0, right_ref), (1, left_ref)):
        @pl.when(me == mids[which])
        def _():
            def unfold(low, carry):
                parts = []
                for source in (low, low + half_tiles):
                    @pl.when(source != me)
                    def _():
                        to_mid(1 - which, source).wait_recv()
                    fold = direct_ref[source]
                    parts.append(jnp.concatenate([fold[:, :half], fold[:, half:]], axis=0))
                dst[block(low), :] = jnp.concatenate(parts, axis=1)
                return carry

            lax.fori_loop(0, half_tiles, unfold, 0)

        @pl.when(me != mids[which])
        def _():
            to_mid(which, me).wait_send()

    def sent(step, carry):
        to_owner((me + step) % tiles, me).wait_send()
        return carry

    lax.fori_loop(1, tiles, sent, 0)

    def arrived(source, carry):
        @pl.when(has_left)
        def _():
            to_side(0, source).wait_send()
            to_side(1, source).wait_recv()

        @pl.when(has_right)
        def _():
            to_side(1, source).wait_send()
            to_side(0, source).wait_recv()

        return carry

    lax.fori_loop(0, half_tiles, arrived, 0)


def radix_sixteen(x):
    c1, c2, c3 = (math.cos(math.pi * n / 8.0) for n in (1, 2, 3))
    s = [x[d] + x[d + 8] for d in range(8)]
    t = [x[d] - x[d + 8] for d in range(8)]
    u = [s[d] + s[d + 4] for d in range(4)]
    v = [s[d] - s[d + 4] for d in range(4)]
    z = [None] * 9
    z[0] = (u[0] + u[2] + (u[1] + u[3]), None)
    z[8] = (u[0] + u[2] - (u[1] + u[3]), None)
    z[4] = (u[0] - u[2], u[3] - u[1])
    less, more = c2 * (v[1] - v[3]), c2 * (v[1] + v[3])
    z[2] = (v[0] + less, -(v[2] + more))
    z[6] = (v[0] - less, v[2] - more)
    a1, a2, a3 = t[1] - t[7], c2 * (t[2] - t[6]), t[3] - t[5]
    b1, b2, b3 = t[1] + t[7], c2 * (t[2] + t[6]), t[3] + t[5]
    p, q = t[0] + a2, c1 * a1 + c3 * a3
    z[1], z[7] = [p + q, None], [p - q, None]
    p, q = t[0] - a2, c3 * a1 - c1 * a3
    z[3], z[5] = [p + q, None], [p - q, None]
    p, q = c3 * b1 + c1 * b3, b2 + t[4]
    z[1][1], z[7][1] = -(p + q), q - p
    p, q = c1 * b1 - c3 * b3, b2 - t[4]
    z[3][1], z[5][1] = -(p + q), q - p
    return z


def cross_kernel(own_ref, left_ref, right_ref, far_ref, pick_ref, scale_ref, out_ref,
                 high_ref, spec_ref, table_ref, load_sem):
    load = pltpu.make_async_copy(far_ref, table_ref, load_sem)
    load.start()
    frames_len, slot_count = own_ref.shape
    span = frames_len // RADIX
    per = span // 2
    step_rows = 16
    half = slot_count // 2

    lane = lax.broadcasted_iota(jnp.int32, (step_rows, slot_count), 1)
    front = lane < half

    def put(k1, part, start, lane0, value):
        if value is not None:
            rows = pl.ds(part * span + start, step_rows)
            high_ref[k1, rows, lane0:lane0 + slot_count] = value.astype(jnp.bfloat16)

    def one_step(step, carry):
        start = pl.multiple_of(step * step_rows, step_rows)
        own, near = [], [None] * RADIX
        for d in range(RADIX):
            own.append(own_ref[pl.ds(d * span + start, step_rows), :].astype(jnp.float32))
        for d in range(RADIX // 2):
            left = left_ref[pl.ds(d * span + start, step_rows), :].astype(jnp.float32)
            right = right_ref[pl.ds(d * span + start, step_rows), :].astype(jnp.float32)
            near[d] = jnp.where(front, left, pltpu.roll(right, half, 1))
            near[d + 8] = jnp.where(front, pltpu.roll(left, half, 1), right)
        for lane0, group in ((0, own), (slot_count, near)):
            for k1, (real, imag) in enumerate(radix_sixteen(group)):
                put(k1, 0, start, lane0, real)
                put(k1, 1, start, lane0, imag)
        return carry

    lax.fori_loop(0, span // step_rows, one_step, 0)

    load.wait()
    for k1 in range(RADIX):
        src = min(k1, RADIX - k1)
        depth = span if k1 % (RADIX // 2) == 0 else 2 * span
        found = jnp.dot(
            table_ref[k1, :, :depth], high_ref[src, :depth, :], preferred_element_type=jnp.float32
        )
        for side in range(2):
            lanes = slice(side * slot_count, (side + 1) * slot_count)
            for part in range(2):
                spec_ref[part, side, pl.ds(k1, per, RADIX), :] = found[part * per:(part + 1) * per, lanes]

    bins = RADIX * per
    width = 256
    pix = pick_ref.shape[0] // 5
    cols = pix // ROWS

    def one_band(band, carry):
        start = pl.multiple_of(band * width, width)
        grids = []
        for part in range(2):
            spec = jnp.concatenate(
                [spec_ref[part, side, pl.ds(start, width), :] for side in range(2)], axis=1
            ).astype(jnp.bfloat16)
            grids.append(lax.dot_general(
                pick_ref[...], spec, (((1,), (1,)), ((), ())), preferred_element_type=jnp.float32
            ))
        real, imag = grids
        own_r, own_i = real[:pix], imag[:pix]
        for which in range(4):
            rows = slice((which + 1) * pix, (which + 2) * pix)
            far_r, far_i = real[rows], imag[rows]
            scale = jnp.concatenate([scale_ref[which]] * (width // 128), axis=1)
            out_r = jnp.sum((own_r * far_r + own_i * far_i).reshape(ROWS, cols, width), axis=0)
            out_i = jnp.sum((own_i * far_r - own_r * far_i).reshape(ROWS, cols, width), axis=0)
            out_ref[:, which, 0, pl.ds(start, width)] = out_r * scale
            out_ref[:, which, 1, pl.ds(start, width)] = out_i * scale
        return carry

    lax.fori_loop(0, bins // width, one_band, 0, unroll=4)


def per_device(table, frames, frame_valid, valid_count, block_map, offsets):
    tile_count = lax.axis_size("tm")
    frame_dev, pixel_count = frames.shape
    tile_pix = pixel_count // tile_count
    tile_width = tile_pix // ROWS
    slot_count = tile_pix // 2
    frames_len = tile_count * frame_dev
    span = frames_len // RADIX
    bins = frames_len // 2
    vmem = pl.BlockSpec(memory_space=pltpu.VMEM)
    own, left, right, pick, scales = pl.pallas_call(
        functools.partial(exchange_kernel, tile_count),
        out_shape=[
            jax.ShapeDtypeStruct((frames_len, slot_count), jnp.bfloat16),
            jax.ShapeDtypeStruct((bins, slot_count), jnp.bfloat16),
            jax.ShapeDtypeStruct((bins, slot_count), jnp.bfloat16),
            jax.ShapeDtypeStruct((5 * tile_pix, tile_pix), jnp.bfloat16),
            jax.ShapeDtypeStruct((offsets.shape[0], tile_width, 128), jnp.float32),
        ],
        in_specs=[pl.BlockSpec(memory_space=pl.ANY)] + [vmem] * 4,
        out_specs=[vmem] * 5,
        scratch_shapes=[
            pltpu.VMEM((frame_dev, pixel_count), jnp.bfloat16),
            pltpu.VMEM((tile_count, tile_pix), jnp.int32),
            pltpu.VMEM((tile_count, frame_dev, slot_count), jnp.bfloat16),
            pltpu.VMEM((2, bins, slot_count), jnp.bfloat16),
            pltpu.VMEM((2, frame_dev // 2, slot_count), jnp.bfloat16),
            pltpu.VMEM((tile_count, frame_dev // 2, slot_count), jnp.bfloat16),
            pltpu.SemaphoreType.DMA((tile_count,)),
            pltpu.SemaphoreType.DMA((tile_count,)),
            pltpu.SemaphoreType.DMA((2, tile_count // 2)),
            pltpu.SemaphoreType.DMA((2, tile_count // 2)),
            pltpu.SemaphoreType.DMA((2,)),
            pltpu.SemaphoreType.DMA((tile_count,)),
            pltpu.SemaphoreType.DMA,
        ],
        compiler_params=pltpu.CompilerParams(
            vmem_limit_bytes=VMEM_LIMIT, collective_id=0, has_side_effects=True
        ),
        name="exchange",
    )(frames, frame_valid[None, :], valid_count[None, :], block_map, offsets.T)
    return pl.pallas_call(
        cross_kernel,
        out_shape=jax.ShapeDtypeStruct((tile_width, offsets.shape[0], 2, bins), jnp.float32),
        scratch_shapes=[
            pltpu.VMEM((RADIX // 2 + 1, 2 * span, 2 * slot_count), jnp.bfloat16),
            pltpu.VMEM((2, 2, bins, slot_count), jnp.float32),
            pltpu.VMEM(table.shape, table.dtype),
            pltpu.SemaphoreType.DMA,
        ],
        in_specs=[vmem] * 3 + [pl.BlockSpec(memory_space=pl.ANY)] + [vmem] * 2,
        out_specs=vmem,
        compiler_params=pltpu.CompilerParams(vmem_limit_bytes=VMEM_LIMIT),
        name="transform_cross",
    )(own, left, right, table, pick, scales)


def solution(mesh):
    def run(frames, frame_valid, valid_count, block_map, offsets):
        table = jnp.asarray(dft_table(frames.shape[0]))
        return jax.shard_map(
            per_device,
            mesh=mesh,
            in_specs=(P(), P("tm", "groups"), P(("groups", "tm")), P("groups"), P("groups", None), P()),
            out_specs=P(("groups", "tm"), None, None, None),
            check_vma=False,
        )(table, frames, frame_valid, valid_count, block_map, offsets)

    return run
```

```python
import functools
import math

import jax
import jax.numpy as jnp
import ml_dtypes
import numpy as np
from jax import lax
from jax.experimental import pallas as pl
from jax.experimental.pallas import tpu as pltpu
from jax.sharding import PartitionSpec as P

ROWS = 16
REACH = 4
RADIX = 16
VMEM_LIMIT = 56 * 1024 * 1024


def dft_table(frames_len):
    span = frames_len // RADIX
    per = span // 2
    j = np.arange(span)
    out = np.zeros((RADIX, 2 * per, 2 * span), np.float64)
    for k1 in range(RADIX):
        bins = k1 + RADIX * np.arange(per)
        angle = (bins[:, None] * j[None, :] % frames_len) * (2.0 * math.pi / frames_len)
        cos, sin = np.cos(angle), np.sin(angle)
        sign = 1.0 if k1 <= RADIX // 2 else -1.0
        out[k1, :per, :span] = cos
        out[k1, :per, span:] = sign * sin
        out[k1, per:, :span] = -sin
        out[k1, per:, span:] = sign * cos
    return (out / math.sqrt(frames_len)).astype(np.float32).astype(ml_dtypes.bfloat16)


def bits(flags):
    return flags.astype(jnp.float32).astype(jnp.bfloat16)


def dot_last(left, right):
    return lax.dot_general(
        left, right, (((1,), (1,)), ((), ())), preferred_element_type=jnp.float32
    )


def number_slots(count_ref, map_ref, slots_ref):
    tiles, tile_pix = map_ref.shape
    width = tile_pix // ROWS
    shift = width.bit_length() - 1
    group = tile_pix // ROWS
    row_idx = lax.broadcasted_iota(jnp.int32, (tile_pix, tile_pix), 0)
    col_idx = lax.broadcasted_iota(jnp.int32, (tile_pix, tile_pix), 1)
    row_high, row_low = row_idx >> shift, row_idx & (width - 1)
    col_high, col_low = col_idx >> shift, col_idx & (width - 1)
    same_tile = row_high == col_high
    same_low = bits(row_low == col_low)
    row_match = row_low == col_high
    before = bits(row_low * ROWS + row_high < col_low * ROWS + col_high)
    slim = lax.broadcasted_iota(jnp.int32, (group, tile_pix), 0)
    lane = lax.broadcasted_iota(jnp.int32, (group, tile_pix), 1)
    tile_pick = bits((lane >> shift) == slim)
    part_idx = lax.broadcasted_iota(jnp.int32, (group, ROWS, tile_pix), 1)
    for first in range(0, tiles, group):
        near_diag = lax.broadcasted_iota(jnp.int32, (group, tiles), 1) == (
            lax.broadcasted_iota(jnp.int32, (group, tiles), 0) + first
        )
        count = jnp.sum(
            jnp.where(near_diag, count_ref[...].astype(jnp.float32), 0.0), axis=1, keepdims=True
        ).astype(jnp.int32)
        pixel = map_ref[first:first + group, :]
        row = jnp.where(lane < count, pixel >> shift, -1)
        col = pixel & (width - 1)
        row_hot = (row[:, None, :] == part_idx).astype(jnp.float32).reshape(tile_pix, tile_pix)
        col_hot = (col[:, None, :] == part_idx).astype(jnp.float32).reshape(tile_pix, tile_pix)
        met = dot_last(row_hot.astype(jnp.bfloat16), col_hot.astype(jnp.bfloat16))
        met = jnp.where(same_tile, met, 0.0).astype(jnp.bfloat16)
        wide = jnp.dot(met, same_low, preferred_element_type=jnp.float32)
        wide = jnp.where(row_match, wide, 0.0).astype(jnp.bfloat16)
        valid = jnp.dot(tile_pick, wide, preferred_element_type=jnp.float32)
        rank = jnp.dot(valid.astype(jnp.bfloat16), before, preferred_element_type=jnp.float32)
        back = jnp.where((lane & (width - 1)) >= width // 2, tile_pix // 2 - count, 0)
        slots_ref[first:first + group, :] = jnp.where(
            valid > 0.5, rank.astype(jnp.int32) + back, -1
        )


def pick_pairs(me, tiles, slots_ref, offsets_ref, pick_ref, scale_ref):
    tile_pix = slots_ref.shape[1]
    width = tile_pix // ROWS
    shift = width.bit_length() - 1
    quarter = tile_pix // 4
    left = slots_ref[pl.ds((me + tiles - 1) % tiles, 1), :]
    own = slots_ref[pl.ds(me, 1), :]
    right = slots_ref[pl.ds((me + 1) % tiles, 1), :]
    left = jnp.where((left >= quarter * 1) & (me > 0), left + quarter, -1)
    right = jnp.where((right >= 0) & (right < quarter) & (me < tiles - 1), right + 3 * quarter, -1)
    row_idx = lax.broadcasted_iota(jnp.int32, (tile_pix, tile_pix), 0)
    col_idx = lax.broadcasted_iota(jnp.int32, (tile_pix, tile_pix), 1)
    sides = [bits(row_idx == ids) for ids in (left, own, right)]
    own_valid = None
    for which in range(5):
        row, col = row_idx >> shift, row_idx & (width - 1)
        if which > 0:
            row = row + offsets_ref[0:1, which - 1:which]
            col = col + offsets_ref[1:2, which - 1:which]
        here = ((row * width + (col & (width - 1))) == col_idx) & (row >= 0) & (row < ROWS)
        conds = (col < 0, (col >= 0) & (col < width), col >= width)
        found = None
        for cond, side in zip(conds, sides):
            term = dot_last(bits(here & cond), side)
            found = term if found is None else found + term
        pick_ref[which * tile_pix:(which + 1) * tile_pix, :] = found.astype(jnp.bfloat16)
        valid = jnp.sum(found, axis=1, keepdims=True)
        if which == 0:
            own_valid = valid
        else:
            both = jnp.broadcast_to(own_valid * valid, (tile_pix, 128)).reshape(ROWS, width, 128)
            scale_ref[which - 1] = 1.0 / jnp.maximum(jnp.sum(both, axis=0), 1.0)
        yield which


def exchange_kernel(tiles, far_ref, keep_ref, count_ref, map_ref, offsets_ref,
                    own_ref, left_ref, right_ref, pick_ref, scale_ref,
                    frames_ref, slots_ref, pack_ref, side_ref, fold_ref, direct_ref,
                    send_sem, recv_sem, halo_send, halo_recv, direct_send, direct_recv,
                    load_sem):
    me = lax.axis_index("tm")
    group = lax.axis_index("groups")
    rows = pack_ref.shape[1]
    slot_count = pack_ref.shape[2]
    tile_pix = slots_ref.shape[1]
    half_tiles = tiles // 2
    half = slot_count // 2
    mesh_id = pl.DeviceIdType.MESH

    load = pltpu.make_async_copy(far_ref, frames_ref, load_sem)
    load.start()
    barrier = pltpu.get_barrier_semaphore()

    def greet(step, carry):
        pl.semaphore_signal(
            barrier, inc=1, device_id=(group, (me + step) % tiles), device_id_type=mesh_id
        )
        return carry

    lax.fori_loop(1, tiles, greet, 0)

    number_slots(count_ref, map_ref, slots_ref)
    keep = jnp.broadcast_to(keep_ref[...].astype(jnp.float32), (slot_count, rows)).T
    slot_idx = lax.broadcasted_iota(jnp.int32, (slot_count, tile_pix), 0)

    def packed(tile):
        pick = bits(slot_idx == slots_ref[pl.ds(tile, 1), :])
        start = pl.multiple_of(tile * tile_pix, tile_pix)
        return (dot_last(frames_ref[:, pl.ds(start, tile_pix)], pick) * keep).astype(jnp.bfloat16)

    def block(source):
        return pl.ds(pl.multiple_of(source * rows, rows), rows)

    def to_owner(tile, source):
        return pltpu.make_async_remote_copy(
            src_ref=pack_ref.at[tile], dst_ref=own_ref.at[block(source)],
            send_sem=send_sem.at[tile], recv_sem=recv_sem.at[source],
            device_id=(group, tile), device_id_type=mesh_id,
        )

    load.wait()
    pl.semaphore_wait(barrier, tiles - 1)

    def send(tile):
        pack_ref[tile] = packed(tile)
        to_owner(tile, me).start()

    send((me + half_tiles) % tiles)

    def send_two(step, carry):
        send((me + half_tiles + step) % tiles)
        send((me + step) % tiles)
        return carry

    lax.fori_loop(1, half_tiles, send_two, 0)
    pack_ref[me] = packed(me)
    own_ref[block(me), :] = pack_ref[me]

    mid = half_tiles - 1
    mids = (mid, mid + 1)

    def to_mid(which, source):
        return pltpu.make_async_remote_copy(
            src_ref=fold_ref.at[which], dst_ref=direct_ref.at[source],
            send_sem=direct_send.at[which], recv_sem=direct_recv.at[source],
            device_id=(group, mids[which]), device_id_type=mesh_id,
        )

    for which in range(2):
        block_there = pack_ref[mids[1 - which]]
        lanes = slice(0, half) if which == 0 else slice(half, slot_count)
        margin = block_there[:, lanes]
        fold_ref[which] = jnp.concatenate([margin[:rows // 2], margin[rows // 2:]], axis=1)

        @pl.when(me != mids[which])
        def _():
            to_mid(which, me).start()

        @pl.when(me == mids[which])
        def _():
            direct_ref[me] = fold_ref[which]


    def to_side(way, source):
        target = (me + tiles - 1) % tiles if way == 0 else (me + 1) % tiles
        dst = right_ref if way == 0 else left_ref
        return pltpu.make_async_remote_copy(
            src_ref=side_ref.at[way, block(source)], dst_ref=dst.at[block(source)],
            send_sem=halo_send.at[way, source], recv_sem=halo_recv.at[way, source],
            device_id=(group, target), device_id_type=mesh_id,
        )

    has_left = (me > 0) & (me != half_tiles)
    has_right = (me < tiles - 1) & (me != half_tiles - 1)

    def forward(step, carry):
        low = (me + tiles - step) % half_tiles
        high = low + half_tiles
        for source in (low, high):
            @pl.when(source != me)
            def _():
                to_owner((me + 1) % tiles, source).wait_recv()
        near, far = own_ref[block(low), :], own_ref[block(high), :]
        side_ref[0, block(low), :] = jnp.concatenate([near[:, :half], far[:, :half]], axis=1)
        side_ref[1, block(low), :] = jnp.concatenate([near[:, half:], far[:, half:]], axis=1)

        @pl.when(has_left)
        def _():
            to_side(0, low).start()

        @pl.when(has_right)
        def _():
            to_side(1, low).start()

        return carry

    started = 0
    for _ in pick_pairs(me, tiles, slots_ref, offsets_ref, pick_ref, scale_ref):
        if started < half_tiles:
            forward(started, 0)
            started += 1
    lax.fori_loop(started, half_tiles, forward, 0)

    @pl.when(me == 0)
    def _():
        left_ref[...] = jnp.zeros_like(left_ref)

    @pl.when(me == tiles - 1)
    def _():
        right_ref[...] = jnp.zeros_like(right_ref)

    for which, dst in ((0, right_ref), (1, left_ref)):
        @pl.when(me == mids[which])
        def _():
            def unfold(low, carry):
                parts = []
                for source in (low, low + half_tiles):
                    @pl.when(source != me)
                    def _():
                        to_mid(1 - which, source).wait_recv()
                    fold = direct_ref[source]
                    parts.append(jnp.concatenate([fold[:, :half], fold[:, half:]], axis=0))
                dst[block(low), :] = jnp.concatenate(parts, axis=1)
                return carry

            lax.fori_loop(0, half_tiles, unfold, 0)

        @pl.when(me != mids[which])
        def _():
            to_mid(which, me).wait_send()

    def sent(step, carry):
        to_owner((me + step) % tiles, me).wait_send()
        return carry

    lax.fori_loop(1, tiles, sent, 0)

    def arrived(source, carry):
        @pl.when(has_left)
        def _():
            to_side(0, source).wait_send()
            to_side(1, source).wait_recv()

        @pl.when(has_right)
        def _():
            to_side(1, source).wait_send()
            to_side(0, source).wait_recv()

        return carry

    lax.fori_loop(0, half_tiles, arrived, 0)


def radix_sixteen(x):
    c1, c2, c3 = (math.cos(math.pi * n / 8.0) for n in (1, 2, 3))
    s = [x[d] + x[d + 8] for d in range(8)]
    t = [x[d] - x[d + 8] for d in range(8)]
    u = [s[d] + s[d + 4] for d in range(4)]
    v = [s[d] - s[d + 4] for d in range(4)]
    z = [None] * 9
    z[0] = (u[0] + u[2] + (u[1] + u[3]), None)
    z[8] = (u[0] + u[2] - (u[1] + u[3]), None)
    z[4] = (u[0] - u[2], u[3] - u[1])
    less, more = c2 * (v[1] - v[3]), c2 * (v[1] + v[3])
    z[2] = (v[0] + less, -(v[2] + more))
    z[6] = (v[0] - less, v[2] - more)
    a1, a2, a3 = t[1] - t[7], c2 * (t[2] - t[6]), t[3] - t[5]
    b1, b2, b3 = t[1] + t[7], c2 * (t[2] + t[6]), t[3] + t[5]
    p, q = t[0] + a2, c1 * a1 + c3 * a3
    z[1], z[7] = [p + q, None], [p - q, None]
    p, q = t[0] - a2, c3 * a1 - c1 * a3
    z[3], z[5] = [p + q, None], [p - q, None]
    p, q = c3 * b1 + c1 * b3, b2 + t[4]
    z[1][1], z[7][1] = -(p + q), q - p
    p, q = c1 * b1 - c3 * b3, b2 - t[4]
    z[3][1], z[5][1] = -(p + q), q - p
    return z


def cross_kernel(own_ref, left_ref, right_ref, far_ref, pick_ref, scale_ref, out_ref,
                 high_ref, spec_ref, table_ref, load_sem):
    load = pltpu.make_async_copy(far_ref, table_ref, load_sem)
    load.start()
    frames_len, slot_count = own_ref.shape
    span = frames_len // RADIX
    per = span // 2
    step_rows = 16
    half = slot_count // 2

    lane = lax.broadcasted_iota(jnp.int32, (step_rows, slot_count), 1)
    front = lane < half

    def put(k1, part, start, lane0, value):
        if value is not None:
            rows = pl.ds(part * span + start, step_rows)
            high_ref[k1, rows, lane0:lane0 + slot_count] = value.astype(jnp.bfloat16)

    def one_step(step, carry):
        start = pl.multiple_of(step * step_rows, step_rows)
        own, near = [], [None] * RADIX
        for d in range(RADIX):
            own.append(own_ref[pl.ds(d * span + start, step_rows), :].astype(jnp.float32))
        for d in range(RADIX // 2):
            left = left_ref[pl.ds(d * span + start, step_rows), :].astype(jnp.float32)
            right = right_ref[pl.ds(d * span + start, step_rows), :].astype(jnp.float32)
            near[d] = jnp.where(front, left, pltpu.roll(right, half, 1))
            near[d + 8] = jnp.where(front, pltpu.roll(left, half, 1), right)
        for lane0, group in ((0, own), (slot_count, near)):
            for k1, (real, imag) in enumerate(radix_sixteen(group)):
                put(k1, 0, start, lane0, real)
                put(k1, 1, start, lane0, imag)
        return carry

    lax.fori_loop(0, span // step_rows, one_step, 0)

    load.wait()
    for k1 in range(RADIX):
        src = min(k1, RADIX - k1)
        depth = span if k1 % (RADIX // 2) == 0 else 2 * span
        found = jnp.dot(
            table_ref[k1, :, :depth], high_ref[src, :depth, :], preferred_element_type=jnp.float32
        )
        for side in range(2):
            lanes = slice(side * slot_count, (side + 1) * slot_count)
            for part in range(2):
                spec_ref[part, side, pl.ds(k1, per, RADIX), :] = found[part * per:(part + 1) * per, lanes]

    bins = RADIX * per
    width = 256
    pix = pick_ref.shape[0] // 5
    cols = pix // ROWS

    def one_band(band, carry):
        start = pl.multiple_of(band * width, width)
        grids = []
        for part in range(2):
            spec = jnp.concatenate(
                [spec_ref[part, side, pl.ds(start, width), :] for side in range(2)], axis=1
            ).astype(jnp.bfloat16)
            grids.append(lax.dot_general(
                pick_ref[...], spec, (((1,), (1,)), ((), ())), preferred_element_type=jnp.float32
            ))
        real, imag = grids
        own_r, own_i = real[:pix], imag[:pix]
        for which in range(4):
            rows = slice((which + 1) * pix, (which + 2) * pix)
            far_r, far_i = real[rows], imag[rows]
            scale = jnp.concatenate([scale_ref[which]] * (width // 128), axis=1)
            out_r = jnp.sum((own_r * far_r + own_i * far_i).reshape(ROWS, cols, width), axis=0)
            out_i = jnp.sum((own_i * far_r - own_r * far_i).reshape(ROWS, cols, width), axis=0)
            out_ref[:, which, 0, pl.ds(start, width)] = out_r * scale
            out_ref[:, which, 1, pl.ds(start, width)] = out_i * scale
        return carry

    lax.fori_loop(0, bins // width, one_band, 0, unroll=4)


def per_device(table, frames, frame_valid, valid_count, block_map, offsets):
    tile_count = lax.axis_size("tm")
    frame_dev, pixel_count = frames.shape
    tile_pix = pixel_count // tile_count
    tile_width = tile_pix // ROWS
    slot_count = tile_pix // 2
    frames_len = tile_count * frame_dev
    span = frames_len // RADIX
    bins = frames_len // 2
    vmem = pl.BlockSpec(memory_space=pltpu.VMEM)
    own, left, right, pick, scales = pl.pallas_call(
        functools.partial(exchange_kernel, tile_count),
        out_shape=[
            jax.ShapeDtypeStruct((frames_len, slot_count), jnp.bfloat16),
            jax.ShapeDtypeStruct((bins, slot_count), jnp.bfloat16),
            jax.ShapeDtypeStruct((bins, slot_count), jnp.bfloat16),
            jax.ShapeDtypeStruct((5 * tile_pix, tile_pix), jnp.bfloat16),
            jax.ShapeDtypeStruct((offsets.shape[0], tile_width, 128), jnp.float32),
        ],
        in_specs=[pl.BlockSpec(memory_space=pl.ANY)] + [vmem] * 4,
        out_specs=[vmem] * 5,
        scratch_shapes=[
            pltpu.VMEM((frame_dev, pixel_count), jnp.bfloat16),
            pltpu.VMEM((tile_count, tile_pix), jnp.int32),
            pltpu.VMEM((tile_count, frame_dev, slot_count), jnp.bfloat16),
            pltpu.VMEM((2, bins, slot_count), jnp.bfloat16),
            pltpu.VMEM((2, frame_dev // 2, slot_count), jnp.bfloat16),
            pltpu.VMEM((tile_count, frame_dev // 2, slot_count), jnp.bfloat16),
            pltpu.SemaphoreType.DMA((tile_count,)),
            pltpu.SemaphoreType.DMA((tile_count,)),
            pltpu.SemaphoreType.DMA((2, tile_count // 2)),
            pltpu.SemaphoreType.DMA((2, tile_count // 2)),
            pltpu.SemaphoreType.DMA((2,)),
            pltpu.SemaphoreType.DMA((tile_count,)),
            pltpu.SemaphoreType.DMA,
        ],
        compiler_params=pltpu.CompilerParams(
            vmem_limit_bytes=VMEM_LIMIT, collective_id=0, has_side_effects=True
        ),
        name="exchange",
    )(frames, frame_valid[None, :], valid_count[None, :], block_map, offsets.T)
    return pl.pallas_call(
        cross_kernel,
        out_shape=jax.ShapeDtypeStruct((tile_width, offsets.shape[0], 2, bins), jnp.float32),
        scratch_shapes=[
            pltpu.VMEM((RADIX // 2 + 1, 2 * span, 2 * slot_count), jnp.bfloat16),
            pltpu.VMEM((2, 2, bins, slot_count), jnp.float32),
            pltpu.VMEM(table.shape, table.dtype),
            pltpu.SemaphoreType.DMA,
        ],
        in_specs=[vmem] * 3 + [pl.BlockSpec(memory_space=pl.ANY)] + [vmem] * 2,
        out_specs=vmem,
        compiler_params=pltpu.CompilerParams(vmem_limit_bytes=VMEM_LIMIT),
        name="transform_cross",
    )(own, left, right, table, pick, scales)


def solution(mesh):
    def run(frames, frame_valid, valid_count, block_map, offsets):
        table = jnp.asarray(dft_table(frames.shape[0]))
        return jax.shard_map(
            per_device,
            mesh=mesh,
            in_specs=(P(), P("tm", "groups"), P(("groups", "tm")), P("groups"), P("groups", None), P()),
            out_specs=P(("groups", "tm"), None, None, None),
            check_vma=False,
        )(table, frames, frame_valid, valid_count, block_map, offsets)

    return run
```
